32 devices in a mesh: pos: 4 (over x, core), head: 4 (over z), chan: 2 (over y).
Axes of the slice: x: 2, y: 2, z: 4, core: 2. Of those that a mesh axis runs over, the one named last changes fastest.
Arguments:
- inputs_saved: bfloat16 [3, 8192, 1536], P(None, ('pos', 'head'), 'chan'), may hold values from -6 to 6
- conv_weight: bfloat16 [3, 3, 1536, 768], P(None, None, 'chan'), may hold values from -0.09375 to 0.09375
- expand_weight: bfloat16 [3, 768, 1536], P(None, None, 'chan'), may hold values from -0.21875 to 0.21875
- head_weight: bfloat16 [1024, 1536], P(('pos', 'head')), may hold values from -1.796875 to 1.796875
- batch_of: int32 [1024], P(('pos', 'head')), may hold values from 0 to 7
- erase_left: bfloat16 [1536, 64], replicated, may hold values from -0.15625 to 0.15625
- erase_right: bfloat16 [1536, 64], replicated, may hold values from -2.09375 to 2.09375
- bin_gradient: bfloat16 [1024, 32], P(('pos', 'head')), may hold values from -6 to 6
- cover_bins: int32 [1024, 32], P(('pos', 'head')), may hold values from 0 to 8191, as said below
Outputs:
- input_grad: bfloat16 [8192, 1536], P(('pos', 'head'), 'chan')
The draws below stay inside these ranges and needn't reach their ends.
Inputs may be any that keep to these rules, and one draw needn't show every extreme that they name: `cover_bins`: of the 2048 entries of the experiments held by one device of pos and head, at most 256 name positions of any one device; in every draw some device's positions are named by exactly 256 entries of every device. Positions may repeat within an experiment.
All inputs are finite; a program needn't handle non-finite values.
Results may differ from the reference program's by a relative error of at most 0.0095.
Values may be sent and summed in bfloat16 or wider, within the bound.
A program may use at most 128 MiB of HBM per device.

```python
import jax
import jax.numpy as jnp
from jax import lax

C = 1536
C2 = 768
KW = 3
LAYERS = 3
BASE_DILATION = 4
BIN_DEV = 512
E_DEV = 64
COV = 32
NB = 8
RANK = 8
GROUP = 16
POSITIONS = 8192
EXPERIMENTS = 1024
ENTRIES = 2048
CAP = 256


def draw_cover_bins(key, part):
    hottest = jax.random.randint(jax.random.fold_in(key, 11), (), 0, GROUP)
    quarter = GROUP // 4
    placing = jnp.arange(GROUP)
    counted = jnp.where(placing < quarter, CAP, jnp.where(placing < 2 * quarter, CAP // 2, CAP // 4))
    bounds = jnp.cumsum(counted)
    slot_of = jnp.searchsorted(bounds, jnp.arange(ENTRIES), side='right')
    order_key = jax.random.fold_in(key, 12)

    def arrange(source):
        shuffled = jax.random.permutation(jax.random.fold_in(order_key, source), GROUP)
        where_hot = jnp.argmax(shuffled == hottest)
        leading = shuffled[0]
        shuffled = shuffled.at[where_hot].set(leading)
        return shuffled.at[0].set(hottest)
    orders = jax.vmap(arrange)(jnp.arange(GROUP))
    targets = orders[:, slot_of]
    offsets = jax.random.randint(jax.random.fold_in(key, 13), (GROUP, ENTRIES), 0, BIN_DEV)
    return (targets * BIN_DEV + offsets).reshape(EXPERIMENTS, COV).astype(jnp.int32)


def plant(result, stream_key, least, top_value):
    extent = result.shape
    place = [jax.random.randint(jax.random.fold_in(stream_key, axis), (), 0, extent[axis]) for axis in range(len(extent))]
    result = result.at[tuple(place)].set(least)
    longest = extent.index(max(extent))
    place[longest] = (place[longest] + 1) % extent[longest]
    return result.at[tuple(place)].set(top_value)


def block_scale(own_key, shape, cuts, smallest, high):
    level = 1.0
    for axis_at, parts in cuts:
        heights = jax.random.uniform(jax.random.fold_in(jax.random.fold_in(own_key, 6), axis_at), (parts,), jnp.float32, smallest / len(cuts), high / len(cuts))
        level = level * jnp.repeat(jnp.exp(heights), shape[axis_at] // parts).reshape((-1,) + (1,) * (len(shape) - 1 - axis_at))
    return level


def bell_draw(own_key, shape, deviation, bound, cuts=(), kind=jnp.bfloat16):
    factor_of = block_scale(own_key, shape, cuts, -0.22, 0.18) if cuts else 1.0
    result = jax.random.normal(own_key, shape, jnp.float32) * deviation * factor_of
    return jnp.minimum(jnp.maximum(result, -bound), bound).astype(kind)


def setup_inputs(seed: int = 0) -> dict:
    streams_of = jax.random.split(jax.random.key(seed), 10)
    return {
        "inputs_saved": bell_draw(streams_of[0], (LAYERS, POSITIONS, C), 1.0, 6.0, ((1, 16), (2, 2))),
        "conv_weight": bell_draw(streams_of[1], (LAYERS, KW, C, C2), (KW * C) ** -0.5, 0.09375, ((2, 2),)),
        "expand_weight": bell_draw(streams_of[2], (LAYERS, C2, C), C2 ** -0.5, 0.21875, ((2, 2),)),
        "head_weight": bell_draw(streams_of[3], (EXPERIMENTS, C), 0.3, 1.796875, ((0, 16),)),
        "batch_of": plant(jax.random.randint(streams_of[4], (EXPERIMENTS,), 0, NB), jax.random.fold_in(streams_of[4], 1), 0, NB - 1).astype(jnp.int32),
        "erase_left": bell_draw(streams_of[5], (C, NB * RANK), C ** -0.5, 0.15625),
        "erase_right": bell_draw(streams_of[6], (C, NB * RANK), 0.35, 2.09375),
        "bin_gradient": bell_draw(streams_of[7], (EXPERIMENTS, COV), 1.0, 6.0, ((0, 16),)),
        "cover_bins": draw_cover_bins(jax.random.fold_in(streams_of[9], 71), 0),
    }


def gelu_value(value):
    return 0.5 * value * (1.0 + jax.scipy.special.erf(value * 0.7071067811865476))


def gelu_slope(value):
    return 0.5 * (1.0 + jax.scipy.special.erf(value * 0.7071067811865476)) + value * jnp.exp(-0.5 * value * value) * 0.3989422804014327


def reference(inputs_saved, conv_weight, expand_weight, head_weight, batch_of, erase_left, erase_right, bin_gradient, cover_bins):
    projected = jnp.dot(head_weight, erase_left, preferred_element_type=jnp.float32)
    columns = jnp.arange(NB * RANK) // RANK
    chosen = (columns[None, :] == batch_of[:, None]).astype(jnp.float32)
    removed_rows = jnp.dot(projected * chosen, erase_right.astype(jnp.float32).T, precision=lax.Precision.HIGHEST)
    head_vectors = (head_weight.astype(jnp.float32) - removed_rows).astype(jnp.bfloat16)

    blocks = EXPERIMENTS // E_DEV
    grad_blocks = bin_gradient.reshape(blocks, E_DEV, COV)
    vector_blocks = head_vectors.reshape(blocks, E_DEV, C)
    bin_blocks = cover_bins.reshape(blocks, E_DEV, COV)

    def add_block(total, piece):
        grads, vectors, places = piece
        contrib = grads.astype(jnp.float32)[:, :, None] * vectors.astype(jnp.float32)[:, None, :]
        return total.at[places.reshape(-1)].add(contrib.reshape(-1, C)), None

    grad, _ = lax.scan(add_block, jnp.zeros((POSITIONS, C), jnp.float32), (grad_blocks, vector_blocks, bin_blocks))

    for block_level in reversed(range(LAYERS)):
        dilation_factor = BASE_DILATION * 2 ** block_level
        saved = inputs_saved[block_level].astype(jnp.float32)
        act = gelu_value(saved).astype(jnp.bfloat16)
        act_pad = jnp.pad(act, ((dilation_factor, dilation_factor), (0, 0)))
        pre = jnp.zeros((POSITIONS, C2), jnp.float32)
        for kernel_tap in range(KW):
            start = kernel_tap * dilation_factor
            pre = pre + jnp.dot(act_pad[start:start + POSITIONS], conv_weight[block_level, kernel_tap], preferred_element_type=jnp.float32)
        grad_in = grad.astype(jnp.bfloat16)
        grad_mid = jnp.dot(grad_in, expand_weight[block_level].T, preferred_element_type=jnp.float32)
        grad_pre = (grad_mid * gelu_slope(pre)).astype(jnp.bfloat16)
        grad_pad = jnp.pad(grad_pre, ((dilation_factor, dilation_factor), (0, 0)))
        grad_act = jnp.zeros((POSITIONS, C), jnp.float32)
        for kernel_tap in range(KW):
            start = (KW - 1 - kernel_tap) * dilation_factor
            grad_act = grad_act + jnp.dot(grad_pad[start:start + POSITIONS], conv_weight[block_level, kernel_tap].T, preferred_element_type=jnp.float32)
        grad = grad + grad_act * gelu_slope(saved)
    return grad.astype(jnp.bfloat16)
```

```python
import jax
import jax.numpy as jnp
from jax import lax
from jax.sharding import PartitionSpec as P

BASE_DILATION = 4
RANK = 8
SEQ = ("pos", "head")


def gelu_value(value):
    return 0.5 * value * (1.0 + jax.scipy.special.erf(value * 0.7071067811865476))


def gelu_slope(value):
    return (
        0.5 * (1.0 + jax.scipy.special.erf(value * 0.7071067811865476))
        + value * jnp.exp(-0.5 * value * value) * 0.3989422804014327
    )


def from_peer(partial):
    count = lax.axis_size("chan")
    pairs = [(i, (i + 1) % count) for i in range(count)]
    return lax.ppermute(partial.astype(jnp.bfloat16), "chan", pairs).astype(jnp.float32)


def per_device(
    inputs_saved,
    conv_weight,
    expand_weight,
    head_weight,
    batch_of,
    erase_left,
    erase_right,
    bin_gradient,
    cover_bins,
):
    members = lax.axis_size(SEQ)
    place = lax.axis_index(SEQ)
    chan_place = lax.axis_index("chan")
    layers, rows, width = inputs_saved.shape
    taps = conv_weight.shape[1]
    dilation = [BASE_DILATION * 2**n for n in range(layers)]
    reach = [sum(dilation[: n + 1]) for n in range(layers)]
    act_reach = [reach[n] + dilation[n] for n in range(layers)]

    entries = jnp.stack([cover_bins.astype(jnp.float32).T, bin_gradient.astype(jnp.float32).T])
    entries = lax.all_gather(entries, SEQ, axis=2, tiled=True)
    projected = jnp.dot(head_weight, erase_left, preferred_element_type=jnp.float32)
    columns = jnp.arange(erase_left.shape[1]) // RANK
    chosen = (columns[None, :] == batch_of[:, None]).astype(jnp.float32)
    right_share = lax.dynamic_slice_in_dim(erase_right, chan_place * width, width, 0)
    weight_share = lax.dynamic_slice_in_dim(head_weight, chan_place * width, width, 1)
    removed_rows = jnp.dot(
        projected * chosen, right_share.astype(jnp.float32).T, precision=lax.Precision.HIGHEST
    )
    vectors = (weight_share.astype(jnp.float32) - removed_rows).astype(jnp.bfloat16)
    vectors = lax.all_gather(vectors, SEQ, axis=0, tiled=True)

    forward = [(i, i + 1) for i in range(members - 1)]
    backward = [(b, a) for a, b in forward]
    low = lax.ppermute(
        jnp.concatenate([inputs_saved[n, rows - act_reach[n] :] for n in range(layers)]), SEQ, forward
    )
    high = lax.ppermute(
        jnp.concatenate([inputs_saved[n, : act_reach[n]] for n in range(layers)]), SEQ, backward
    )
    around, slopes = [], []
    start = 0
    for n in range(layers):
        stop = start + act_reach[n]
        around.append(jnp.concatenate([low[start:stop], inputs_saved[n], high[start:stop]]))
        start = stop

    for n in range(layers):
        size = rows + 2 * reach[n]
        act = gelu_value(around[n].astype(jnp.float32)).astype(jnp.bfloat16)
        wide = jnp.concatenate(
            [act[t * dilation[n] : t * dilation[n] + size] for t in range(taps)], axis=1
        )
        weight = conv_weight[n].reshape(taps * width, conv_weight.shape[3])
        part = jnp.dot(wide, weight, preferred_element_type=jnp.float32)
        position = place * rows - reach[n] + jnp.arange(size)
        inside = (position >= 0) & (position < members * rows)
        slopes.append((part, inside))

    top = layers - 1
    position = (place * rows - reach[top] + jnp.arange(rows + 2 * reach[top])).astype(jnp.float32)
    spread = jnp.sum(
        jnp.where(entries[0][:, None, :] == position[None, :, None], entries[1][:, None, :], 0.0),
        axis=0,
    ).astype(jnp.bfloat16)
    grad = jnp.dot(spread, vectors, preferred_element_type=jnp.float32)

    peers = [None] * layers
    for n in reversed(range(layers)):
        peers[n] = from_peer(slopes[n][0])

    for n in reversed(range(layers)):
        size = rows + 2 * (reach[n] - dilation[n])
        mid_part = lax.dot_general(
            grad.astype(jnp.bfloat16),
            expand_weight[n],
            (((1,), (1,)), ((), ())),
            preferred_element_type=jnp.float32,
        )
        part, inside = slopes[n]
        slope = jnp.where(inside[:, None], gelu_slope(part + peers[n]), 0.0)
        grad_pre = ((mid_part + from_peer(mid_part)) * slope).astype(jnp.bfloat16)
        grad_act = jnp.zeros((size, width), jnp.float32)
        for t in range(taps):
            first = (taps - 1 - t) * dilation[n]
            grad_act = grad_act + lax.dot_general(
                grad_pre[first : first + size],
                conv_weight[n, t],
                (((1,), (1,)), ((), ())),
                preferred_element_type=jnp.float32,
            )
        saved = around[n][2 * dilation[n] : 2 * dilation[n] + size].astype(jnp.float32)
        grad = grad[dilation[n] : dilation[n] + size] + grad_act * gelu_slope(saved)
    return grad.astype(jnp.bfloat16)


def solution(mesh):
    return jax.shard_map(
        per_device,
        mesh=mesh,
        in_specs=(
            P(None, ("pos", "head"), "chan"),
            P(None, None, "chan", None),
            P(None, None, "chan"),
            P(("pos", "head"), None),
            P(("pos", "head")),
            P(),
            P(),
            P(("pos", "head"), None),
            P(("pos", "head"), None),
        ),
        out_specs=P(("pos", "head"), "chan"),
        check_vma=False,
    )
```

```python
import functools

import jax
import jax.numpy as jnp
from jax import lax
from jax.experimental import pallas as pl
from jax.experimental.pallas import tpu as pltpu
from jax.sharding import PartitionSpec as P

BASE_DILATION = 4
RANK = 8
SEQ = ("pos", "head")
MESH = pl.DeviceIdType.MESH
BF = jnp.bfloat16
F32 = jnp.float32
TILE = 256
STEP = 16
NT = (((1,), (1,)), ((), ()))


def gelu_value(value):
    return 0.5 * value * (1.0 + lax.erf(value * 0.7071067811865476))


def gelu_slope(value):
    return (
        0.5 * (1.0 + lax.erf(value * 0.7071067811865476))
        + value * jnp.exp(-0.5 * value * value) * 0.3989422804014327
    )


def up(value, unit):
    return -(-value // unit) * unit


def frames(layers):
    wide, out, saved, before = [], [], [], 0
    for n in range(layers):
        dilation = BASE_DILATION * 2**n
        out.append(before)
        before = up(before + dilation, 8)
        wide.append(before)
        saved.append(up(before + dilation, 16))
    return wide, out, saved


def kernel(
    layers, rows, width, inner, taps, npos, nhead, exps,
    inputs_ref, conv_ref, expand_ref, pay_ref,
    out_ref,
    sv0, sv1, sv2, conv, expand, vall, sbuf, actf, aw, pp, ps, pr, mp, ms, mr,
    sp, ss, ga, gb, acc, gradbf, gpf, gpw,
    load_sem, own_sem, halo_s, halo_r, s1, r1, s2p, r2p, s2x, r2x, s3, r3, ps_s, ps_r, ms_s, ms_r,
):
    sv = [sv0, sv1, sv2]
    wide, outs, saved = frames(layers)
    dil = [BASE_DILATION * 2**n for n in range(layers)]
    members = npos * nhead
    p, h = lax.axis_index("pos"), lax.axis_index("head")
    peer = {"chan": 1 - lax.axis_index("chan")}
    place = p * nhead + h
    after = lax.rem(place + 1, members)
    ahead = lax.rem(place + members - 1, members)
    follow = {"pos": after // nhead, "head": lax.rem(after, nhead)}
    precede = {"pos": ahead // nhead, "head": lax.rem(ahead, nhead)}
    mate = p + 1 - 2 * lax.rem(p, 2)
    partner = {"pos": mate}
    nx = npos // 2
    ct_n, jt_n = width // TILE, inner // TILE

    def remote(src, dst, send, recv, device):
        return pltpu.make_async_remote_copy(
            src_ref=src, dst_ref=dst, send_sem=send, recv_sem=recv, device_id=device, device_id_type=MESH
        )

    def head_of(dh):
        return lax.rem(h + nhead - dh, nhead)

    def pos_of(start, dx):
        return lax.rem(start + npos - 2 * dx, npos)

    loads = {}
    at = 0
    for n in reversed(range(layers)):
        loads["saved", n] = pltpu.make_async_copy(
            inputs_ref.at[n], sv[n].at[pl.ds(saved[n], rows)], load_sem.at[at]
        )
        loads["conv", n] = pltpu.make_async_copy(conv_ref.at[n], conv.at[n], load_sem.at[at + 1])
        loads["expand", n] = pltpu.make_async_copy(expand_ref.at[n], expand.at[n], load_sem.at[at + 2])
        at += 3
    own = pltpu.make_async_copy(pay_ref, vall.at[p, h], own_sem)
    own.start()
    loads["saved", layers - 1].start()
    loads["conv", layers - 1].start()

    barrier = pltpu.get_barrier_semaphore()
    known = [follow, precede, peer, partner]
    known += [{"head": lax.rem(h + dh, nhead)} for dh in range(1, nhead)]
    known += [{"pos": lax.rem(p + 2 * dx, npos)} for dx in range(1, nx)]
    for device in known:
        pl.semaphore_signal(barrier, inc=1, device_id=device, device_id_type=MESH)
    pl.semaphore_wait(barrier, len(known))

    halos = {}
    for n in reversed(range(layers)):
        k = saved[n]
        halos[n] = [
            remote(inputs_ref.at[n, pl.ds(rows - k, k)], sv[n].at[pl.ds(0, k)],
                   halo_s.at[n, 0], halo_r.at[n, 0], follow),
            remote(inputs_ref.at[n, pl.ds(0, k)], sv[n].at[pl.ds(rows + k, k)],
                   halo_s.at[n, 1], halo_r.at[n, 1], precede),
        ]
    for copy in halos[layers - 1]:
        copy.start()
    first = [
        remote(pay_ref, vall.at[p, h], s1.at[dh], r1.at[dh], {"head": lax.rem(h + dh, nhead)})
        for dh in range(1, nhead)
    ]
    for copy in first:
        copy.start()
    for n in reversed(range(layers - 1)):
        for copy in halos[n]:
            copy.start()
    for n in reversed(range(layers)):
        if n < layers - 1:
            loads["saved", n].start()
            loads["conv", n].start()
        loads["expand", n].start()

    def inside(start, count):
        spot = place * rows + start + lax.broadcasted_iota(jnp.int32, (count, TILE), 0)
        return (spot >= 0) & (spot < members * rows)

    def make_pre(n, push):
        size = rows + 2 * wide[n]
        loads["saved", n].wait()
        for copy in halos[n]:
            copy.wait()

        def activate(r, _):
            place_at = pl.ds(pl.multiple_of(r * STEP, STEP), STEP)
            keep = inside(r * STEP - saved[n], STEP)
            for ct in range(ct_n):
                value = sv[n][place_at, ct * TILE : (ct + 1) * TILE].astype(F32)
                actf[ct, place_at, :] = jnp.where(keep, gelu_value(value), 0.0)
            return 0

        lax.fori_loop(0, (rows + 2 * saved[n]) // STEP, activate, 0)
        for t in range(taps):
            begin = saved[n] - wide[n] + (t - 1) * dil[n]
            for ct in range(ct_n):
                aw[t * ct_n + ct, 0:size, :] = actf[ct, begin : begin + size, :].astype(BF)
        loads["conv", n].wait()

        def column(jt, _):
            cols = pl.ds(pl.multiple_of(jt * TILE, TILE), TILE)
            total = None
            for t in range(taps):
                for ct in range(ct_n):
                    term = jnp.dot(
                        aw[t * ct_n + ct, 0:size, :],
                        conv[n, t, ct * TILE : (ct + 1) * TILE, cols],
                        preferred_element_type=F32,
                    )
                    total = term if total is None else total + term
            pp[n, jt, 0:size, :] = total
            ps[n, jt, 0:size, :] = total.astype(BF)
            if push:
                pre_copy(n, jt).start()
            return 0

        lax.fori_loop(0, jt_n, column, 0)

    def pre_copy(n, jt):
        size = rows + 2 * wide[n]
        return remote(ps.at[n, jt, pl.ds(0, size)], pr.at[n, jt, pl.ds(0, size)],
                      ps_s.at[n, jt], ps_r.at[n, jt], peer)

    def mid_copy(n, jt):
        size = rows + 2 * wide[n]
        return remote(ms.at[n, jt, pl.ds(0, size)], mr.at[n, jt, pl.ds(0, size)],
                      ms_s.at[n, jt], ms_r.at[n, jt], peer)

    top = layers - 1
    make_pre(top, True)

    own.wait()
    to_mate, to_x = [], []
    for dh in range(nhead):
        if dh:
            first[dh - 1].wait()
        block = vall.at[p, head_of(dh)]
        for dx in range(1, nx):
            copy = remote(block, block, s2x.at[dx, dh], r2x.at[dx, dh], {"pos": lax.rem(p + 2 * dx, npos)})
            copy.start()
            to_x.append((dx, dh, copy))
        copy = remote(block, block, s2p.at[dh], r2p.at[dh], partner)
        copy.start()
        to_mate.append(copy)

    if layers > 1:
        make_pre(top - 1, True)

    size_top = rows + 2 * wide[top]

    def clear(r, _):
        at_rows = pl.ds(pl.multiple_of(r * STEP, STEP), STEP)
        for ct in range(ct_n):
            ga[ct, at_rows, :] = jnp.zeros((STEP, TILE), F32)
        return 0

    lax.fori_loop(0, size_top // STEP, clear, 0)
    lanes = 2 * exps
    part_rows = size_top // 3

    def add_slab(slab):
        def pair(i, _):
            values = []
            for side in range(2):
                a = 2 * i + side
                words = vall[slab, a, :, width : width + lanes].astype(F32)
                spots = words[0:16] * 256.0 + words[16:32]
                heights = words[32:48]
                for rt in range(3):
                    line = (place * rows - wide[top] + rt * part_rows).astype(F32)
                    row = line + lax.broadcasted_iota(jnp.int32, (part_rows, lanes), 0).astype(F32)
                    found = jnp.zeros((part_rows, lanes), F32)
                    for k in range(16):
                        found = found + jnp.where(spots[k : k + 1] == row, heights[k : k + 1], 0.0)
                    sbuf[rt * part_rows : (rt + 1) * part_rows, side * lanes : (side + 1) * lanes] = (
                        found.astype(BF)
                    )
                block = vall[slab, a, :, 0:width]
                values += [block, block]
            right = jnp.concatenate(values, axis=0)
            for ct in range(ct_n):
                ga[ct, 0:size_top, :] += jnp.dot(
                    sbuf[...], right[:, ct * TILE : (ct + 1) * TILE], preferred_element_type=F32
                )
            return 0

        lax.fori_loop(0, nhead // 2, pair, 0)

    add_slab(p)
    onward = []
    for dx, dh, copy in to_x:
        copy.wait()
        block = vall.at[pos_of(p, dx), head_of(dh)]
        copy = remote(block, block, s3.at[dx, dh], r3.at[dx, dh], partner)
        copy.start()
        onward.append(copy)
    for copy in to_mate:
        copy.wait()
    add_slab(mate)
    for dx in range(1, nx):
        add_slab(pos_of(p, dx))
    for copy in onward:
        copy.wait()
    for dx in range(1, nx):
        add_slab(pos_of(mate, dx))

    grads = [ga, gb]
    for n in reversed(range(layers)):
        now, later = grads[(top - n) % 2], grads[(top - n + 1) % 2]
        size = rows + 2 * wide[n]
        size_out = rows + 2 * outs[n]
        shift = wide[n] - outs[n]

        def lower(r, _):
            at_rows = pl.ds(pl.multiple_of(r * STEP, STEP), STEP)
            for ct in range(ct_n):
                gradbf[ct, at_rows, :] = now[ct, at_rows, :].astype(BF)
            return 0

        lax.fori_loop(0, size // STEP, lower, 0)
        loads["expand", n].wait()

        def middle(jt, _):
            js = pl.ds(pl.multiple_of(jt * TILE, TILE), TILE)
            total = None
            for ct in range(ct_n):
                term = lax.dot_general(
                    gradbf[ct, 0:size, :], expand[n, js, ct * TILE : (ct + 1) * TILE], NT,
                    preferred_element_type=F32,
                )
                total = term if total is None else total + term
            mp[jt, 0:size, :] = total
            ms[n, jt, 0:size, :] = total.astype(BF)
            mid_copy(n, jt).start()
            return 0

        lax.fori_loop(0, jt_n, middle, 0)
        if n == top:
            make_pre(0, True)

        def steepness(r, _):
            from_rows = pl.ds(pl.multiple_of(r * STEP, STEP) + (saved[n] - outs[n]) // STEP * STEP, STEP)
            at_rows = pl.ds(pl.multiple_of(r * STEP, STEP), STEP)
            for ct in range(ct_n):
                value = sv[n][from_rows, ct * TILE : (ct + 1) * TILE].astype(F32)
                ss[ct, at_rows, :] = gelu_slope(value)
            return 0

        skew = (saved[n] - outs[n]) % STEP
        lax.fori_loop(0, up(size_out + skew, STEP) // STEP, steepness, 0)
        for jt in range(jt_n):
            pre_copy(n, jt).wait()

        def slope_of_pre(r, _):
            at_rows = pl.ds(pl.multiple_of(r * STEP, STEP), STEP)
            keep = inside(r * STEP - wide[n], STEP)
            for jt in range(jt_n):
                value = pp[n, jt, at_rows, :] + pr[n, jt, at_rows, :].astype(F32)
                sp[jt, at_rows, :] = jnp.where(keep, gelu_slope(value), 0.0)
            return 0

        lax.fori_loop(0, size // STEP, slope_of_pre, 0)

        for jt in range(jt_n):
            mid_copy(n, jt).wait()
            gpf[0:size, :] = (mp[jt, 0:size, :] + mr[n, jt, 0:size, :].astype(F32)) * sp[jt, 0:size, :]
            for t in range(taps):
                begin = shift + (1 - t) * dil[n]
                gpw[t, 0:size_out, :] = gpf[begin : begin + size_out, :].astype(BF)

            def back(ct, _):
                at_channels = pl.ds(pl.multiple_of(ct * TILE, TILE), TILE)
                total = None
                for t in range(taps):
                    term = lax.dot_general(
                        gpw[t, 0:size_out, :], conv[n, t, at_channels, jt * TILE : (jt + 1) * TILE], NT,
                        preferred_element_type=F32,
                    )
                    total = term if total is None else total + term
                if jt == 0:
                    acc[ct, 0:size_out, :] = total
                else:
                    acc[ct, 0:size_out, :] += total
                return 0

            lax.fori_loop(0, ct_n, back, 0)

        def step_on(r, _):
            at_rows = pl.ds(pl.multiple_of(r * STEP, STEP), STEP)
            from_rows = pl.ds(pl.multiple_of(r * STEP + shift, 8), STEP)
            slope_rows = pl.ds(pl.multiple_of(r * STEP + skew, 8), STEP)
            for ct in range(ct_n):
                total = now[ct, from_rows, :] + acc[ct, at_rows, :] * ss[ct, slope_rows, :]
                if n:
                    later[ct, at_rows, :] = total
                else:
                    out_ref[at_rows, ct * TILE : (ct + 1) * TILE] = total.astype(BF)
            return 0

        lax.fori_loop(0, size_out // STEP, step_on, 0)


def per_device(
    inputs_saved,
    conv_weight,
    expand_weight,
    head_weight,
    batch_of,
    erase_left,
    erase_right,
    bin_gradient,
    cover_bins,
):
    npos, nhead = lax.axis_size("pos"), lax.axis_size("head")
    chan_place = lax.axis_index("chan")
    layers, rows, width = inputs_saved.shape
    taps, inner = conv_weight.shape[1], conv_weight.shape[3]
    exps, cover = cover_bins.shape

    projected = jnp.dot(head_weight, erase_left, preferred_element_type=F32)
    columns = jnp.arange(erase_left.shape[1]) // RANK
    chosen = (columns[None, :] == batch_of[:, None]).astype(F32)
    right_share = lax.dynamic_slice_in_dim(erase_right, chan_place * width, width, 0)
    weight_share = lax.dynamic_slice_in_dim(head_weight, chan_place * width, width, 1)
    removed_rows = jnp.dot(
        projected * chosen, right_share.astype(F32).T, precision=lax.Precision.HIGHEST
    )
    vectors = (weight_share.astype(F32) - removed_rows).astype(BF)

    def fold(array):
        return array.astype(BF).T.reshape(2, cover // 2, exps).transpose(1, 0, 2).reshape(cover // 2, 2 * exps)

    words = jnp.concatenate(
        [fold(cover_bins // 256), fold(cover_bins % 256), fold(bin_gradient), jnp.zeros((exps - 3 * cover // 2, 2 * exps), BF)]
    )
    pay = jnp.concatenate([vectors, words], axis=1)

    wide, _, saved = frames(layers)
    most = rows + 2 * wide[-1]
    span = rows + 2 * saved[-1]
    ct_n, jt_n = width // TILE, inner // TILE
    nx = npos // 2
    sems = pltpu.SemaphoreType.DMA
    return pl.pallas_call(
        functools.partial(kernel, layers, rows, width, inner, taps, npos, nhead, exps),
        out_shape=jax.ShapeDtypeStruct((rows, width), BF),
        in_specs=[pl.BlockSpec(memory_space=pl.ANY)] * 4,
        out_specs=pl.BlockSpec(memory_space=pltpu.VMEM),
        scratch_shapes=[
            *[pltpu.VMEM((rows + 2 * k, width), BF) for k in saved],
            pltpu.VMEM(conv_weight.shape, BF),
            pltpu.VMEM(expand_weight.shape, BF),
            pltpu.VMEM((npos, nhead, *pay.shape), BF),
            pltpu.VMEM((most, 4 * exps), BF),
            pltpu.VMEM((ct_n, span, TILE), F32),
            pltpu.VMEM((taps * ct_n, most, TILE), BF),
            pltpu.VMEM((layers, jt_n, most, TILE), F32),
            pltpu.VMEM((layers, jt_n, most, TILE), BF),
            pltpu.VMEM((layers, jt_n, most, TILE), BF),
            pltpu.VMEM((jt_n, most, TILE), F32),
            pltpu.VMEM((layers, jt_n, most, TILE), BF),
            pltpu.VMEM((layers, jt_n, most, TILE), BF),
            pltpu.VMEM((jt_n, most, TILE), F32),
            pltpu.VMEM((ct_n, most, TILE), F32),
            pltpu.VMEM((ct_n, most, TILE), F32),
            pltpu.VMEM((ct_n, most, TILE), F32),
            pltpu.VMEM((ct_n, most, TILE), F32),
            pltpu.VMEM((ct_n, most, TILE), BF),
            pltpu.VMEM((most, TILE), F32),
            pltpu.VMEM((taps, most, TILE), BF),
            sems((3 * layers,)),
            sems,
            sems((layers, 2)), sems((layers, 2)),
            sems((nhead,)), sems((nhead,)),
            sems((nhead,)), sems((nhead,)),
            sems((nx, nhead)), sems((nx, nhead)),
            sems((nx, nhead)), sems((nx, nhead)),
            sems((layers, jt_n)), sems((layers, jt_n)),
            sems((layers, jt_n)), sems((layers, jt_n)),
        ],
        compiler_params=pltpu.CompilerParams(
            collective_id=0, has_side_effects=True, vmem_limit_bytes=63 * 2**20
        ),
    )(inputs_saved, conv_weight, expand_weight, pay)


def solution(mesh):
    return jax.shard_map(
        per_device,
        mesh=mesh,
        in_specs=(
            P(None, ("pos", "head"), "chan"),
            P(None, None, "chan", None),
            P(None, None, "chan"),
            P(("pos", "head"), None),
            P(("pos", "head")),
            P(),
            P(),
            P(("pos", "head"), None),
            P(("pos", "head"), None),
        ),
        out_specs=P(("pos", "head"), "chan"),
        check_vma=False,
    )
```

```python
import functools

import jax
import jax.numpy as jnp
from jax import lax
from jax.experimental import pallas as pl
from jax.experimental.pallas import tpu as pltpu
from jax.sharding import PartitionSpec as P

BASE_DILATION = 4
RANK = 8
SEQ = ("pos", "head")
MESH = pl.DeviceIdType.MESH
BF = jnp.bfloat16
F32 = jnp.float32
TILE = 256
STEP = 16
LANES = 128
STREAMS = 2
NT = (((1,), (1,)), ((), ()))


def gelu_value(value):
    return 0.5 * value * (1.0 + lax.erf(value * 0.7071067811865476))


def gelu_slope(value):
    return (
        0.5 * (1.0 + lax.erf(value * 0.7071067811865476))
        + value * jnp.exp(-0.5 * value * value) * 0.3989422804014327
    )


def up(value, unit):
    return -(-value // unit) * unit


def frames(layers):
    wide, out, saved, before = [], [], [], 0
    for n in range(layers):
        dilation = BASE_DILATION * 2**n
        out.append(before)
        before = up(before + dilation, 8)
        wide.append(before)
        saved.append(up(before + dilation, 16))
    return wide, out, saved


def kernel(
    layers, rows, width, inner, taps, npos, nhead, exps,
    inputs_ref, conv_ref, expand_ref, pay_ref,
    out_ref,
    sv0, sv1, sv2, conv, expand, vall, sbuf, actf, aw, pp, ps, pr, mp, ms, mr, go, gr,
    ss, top_grad, ga, gb, acc, gradbf, gpf,
    load_sem, own_sem, halo_s, halo_r, s1, r1, s2p, r2p, s2x, r2x, s3, r3,
    ps_s, ps_r, ms_s, ms_r, go_s, go_r,
):
    sv = [sv0, sv1, sv2]
    wide, outs, saved = frames(layers)
    dil = [BASE_DILATION * 2**n for n in range(layers)]
    members = npos * nhead
    p, h = lax.axis_index("pos"), lax.axis_index("head")
    mine = lax.axis_index("chan")
    peer = {"chan": 1 - mine}
    place = p * nhead + h
    after = lax.rem(place + 1, members)
    ahead = lax.rem(place + members - 1, members)
    follow = {"pos": after // nhead, "head": lax.rem(after, nhead)}
    precede = {"pos": ahead // nhead, "head": lax.rem(ahead, nhead)}
    mate = p + 1 - 2 * lax.rem(p, 2)
    partner = {"pos": mate}
    nx = npos // 2
    ct_n, half = width // TILE, inner // 2
    jt_n = half // LANES
    halves = [pl.multiple_of((1 - mine) * half, LANES), pl.multiple_of(mine * half, LANES)]

    def remote(src, dst, send, recv, device):
        return pltpu.make_async_remote_copy(
            src_ref=src, dst_ref=dst, send_sem=send, recv_sem=recv, device_id=device, device_id_type=MESH
        )

    def head_of(dh):
        return lax.rem(h + nhead - dh, nhead)

    def pos_of(start, dx):
        return lax.rem(start + npos - 2 * dx, npos)

    loads = {}
    at = 0
    for n in reversed(range(layers)):
        loads["saved", n] = [
            pltpu.make_async_copy(inputs_ref.at[n], sv[n].at[pl.ds(saved[n], rows)], load_sem.at[at])
        ]
        at += 1
        loads["conv", n], loads["expand", n] = [], []
        for side in range(2):
            for t in range(taps):
                loads["conv", n].append(
                    pltpu.make_async_copy(
                        conv_ref.at[n, t, :, pl.ds(halves[side], half)],
                        conv.at[n, side, :, pl.ds(t * half, half)],
                        load_sem.at[at],
                    )
                )
                at += 1
            loads["expand", n].append(
                pltpu.make_async_copy(
                    expand_ref.at[n, pl.ds(halves[side], half)], expand.at[n, side], load_sem.at[at]
                )
            )
            at += 1

    def load(kind, n):
        for copy in loads[kind, n]:
            copy.start()

    def loaded(kind, n):
        for copy in loads[kind, n]:
            copy.wait()

    own = pltpu.make_async_copy(pay_ref, vall.at[p, h], own_sem)
    own.start()
    load("saved", layers - 1)
    load("conv", layers - 1)

    barrier = pltpu.get_barrier_semaphore()
    known = [follow, precede, peer, partner]
    known += [{"head": lax.rem(h + dh, nhead)} for dh in range(1, nhead)]
    known += [{"pos": lax.rem(p + 2 * dx, npos)} for dx in range(1, nx)]
    for device in known:
        pl.semaphore_signal(barrier, inc=1, device_id=device, device_id_type=MESH)
    pl.semaphore_wait(barrier, len(known))

    halos = {}
    for n in reversed(range(layers)):
        k = saved[n]
        halos[n] = [
            remote(inputs_ref.at[n, pl.ds(rows - k, k)], sv[n].at[pl.ds(0, k)],
                   halo_s.at[n, 0], halo_r.at[n, 0], follow),
            remote(inputs_ref.at[n, pl.ds(0, k)], sv[n].at[pl.ds(rows + k, k)],
                   halo_s.at[n, 1], halo_r.at[n, 1], precede),
        ]
    for copy in halos[layers - 1]:
        copy.start()
    first = [
        remote(pay_ref, vall.at[p, h], s1.at[dh], r1.at[dh], {"head": lax.rem(h + dh, nhead)})
        for dh in range(1, nhead)
    ]
    for copy in first:
        copy.start()
    for n in reversed(range(layers - 1)):
        for copy in halos[n]:
            copy.start()
    for n in reversed(range(layers)):
        if n < layers - 1:
            load("saved", n)
            load("conv", n)
        load("expand", n)

    def inside(start, count, lanes):
        spot = place * rows + start + lax.broadcasted_iota(jnp.int32, (count, lanes), 0)
        return (spot >= 0) & (spot < members * rows)

    def make_pre(n):
        size = rows + 2 * wide[n]
        loaded("saved", n)
        for copy in halos[n]:
            copy.wait()

        def activate(r, _):
            place_at = pl.ds(pl.multiple_of(r * STEP, STEP), STEP)
            keep = inside(r * STEP - saved[n], STEP, TILE)
            for ct in range(ct_n):
                value = sv[n][place_at, ct * TILE : (ct + 1) * TILE].astype(F32)
                actf[ct, place_at, :] = jnp.where(keep, gelu_value(value), 0.0)
            return 0

        lax.fori_loop(0, (rows + 2 * saved[n]) // STEP, activate, 0)
        for t in range(taps):
            begin = saved[n] - wide[n] + (t - 1) * dil[n]
            for ct in range(ct_n):
                aw[t * ct_n + ct, 0:size, :] = actf[ct, begin : begin + size, :].astype(BF)
        loaded("conv", n)

        for side in range(2):
            total = None
            for t in range(taps):
                for ct in range(ct_n):
                    term = jnp.dot(
                        aw[t * ct_n + ct, 0:size, :],
                        conv[n, side, ct * TILE : (ct + 1) * TILE, t * half : (t + 1) * half],
                        preferred_element_type=F32,
                    )
                    total = term if total is None else total + term
            if side == 0:
                ps[n, 0:size, :] = total.astype(BF)
                pre_copy(n).start()
            else:
                pp[n, 0:size, :] = total

    def pre_copy(n):
        size = pl.ds(0, rows + 2 * wide[n])
        return remote(ps.at[n, size], pr.at[n, size], ps_s.at[n], ps_r.at[n], peer)

    def mid_copy(n, s, jt):
        size = pl.ds(0, part + 2 * wide[n])
        return remote(ms.at[n, s, jt, size], mr.at[n, s, jt, size], ms_s.at[n, s, jt], ms_r.at[n, s, jt], peer)

    def back_copy(n, s, jt):
        size = pl.ds(0, part + 2 * wide[n])
        return remote(go.at[n, s, jt, size], gr.at[n, s, jt, size], go_s.at[n, s, jt], go_r.at[n, s, jt], peer)

    part = rows // STREAMS
    top = layers - 1
    make_pre(top)

    own.wait()
    to_mate, to_x = [], []
    for dh in range(nhead):
        if dh:
            first[dh - 1].wait()
        block = vall.at[p, head_of(dh)]
        for dx in range(1, nx):
            copy = remote(block, block, s2x.at[dx, dh], r2x.at[dx, dh], {"pos": lax.rem(p + 2 * dx, npos)})
            copy.start()
            to_x.append((dx, dh, copy))
        copy = remote(block, block, s2p.at[dh], r2p.at[dh], partner)
        copy.start()
        to_mate.append(copy)

    if layers > 1:
        make_pre(top - 1)

    size_top = rows + 2 * wide[top]

    def clear(r, _):
        at_rows = pl.ds(pl.multiple_of(r * STEP, STEP), STEP)
        for ct in range(ct_n):
            top_grad[ct, at_rows, :] = jnp.zeros((STEP, TILE), F32)
        return 0

    lax.fori_loop(0, size_top // STEP, clear, 0)
    lanes = 2 * exps
    part_rows = size_top // 3

    def add_slab(slab):
        def pair(i, _):
            values = []
            for side in range(2):
                a = 2 * i + side
                words = vall[slab, a, :, width : width + lanes].astype(F32)
                spots = words[0:16] * 256.0 + words[16:32]
                heights = words[32:48]
                for rt in range(3):
                    line = (place * rows - wide[top] + rt * part_rows).astype(F32)
                    row = line + lax.broadcasted_iota(jnp.int32, (part_rows, lanes), 0).astype(F32)
                    found = jnp.zeros((part_rows, lanes), F32)
                    for k in range(16):
                        found = found + jnp.where(spots[k : k + 1] == row, heights[k : k + 1], 0.0)
                    sbuf[rt * part_rows : (rt + 1) * part_rows, side * lanes : (side + 1) * lanes] = (
                        found.astype(BF)
                    )
                block = vall[slab, a, :, 0:width]
                values += [block, block]
            right = jnp.concatenate(values, axis=0)
            for ct in range(ct_n):
                top_grad[ct, 0:size_top, :] += jnp.dot(
                    sbuf[...], right[:, ct * TILE : (ct + 1) * TILE], preferred_element_type=F32
                )
            return 0

        lax.fori_loop(0, nhead // 2, pair, 0)

    add_slab(p)
    onward = []
    for dx, dh, copy in to_x:
        copy.wait()
        block = vall.at[pos_of(p, dx), head_of(dh)]
        copy = remote(block, block, s3.at[dx, dh], r3.at[dx, dh], partner)
        copy.start()
        onward.append(copy)
    for copy in to_mate:
        copy.wait()
    add_slab(mate)
    for n in reversed(range(top - 1)):
        make_pre(n)
    for dx in range(1, nx):
        add_slab(pos_of(p, dx))
    for copy in onward:
        copy.wait()
    for dx in range(1, nx):
        add_slab(pos_of(mate, dx))

    grads = [ga, gb]

    def grad_of(n, s):
        if n == top:
            return lambda ct, start, count: top_grad[ct, pl.ds(s * part + start, count), :]
        held = grads[(top - n) % 2]
        return lambda ct, start, count: held[s, ct, pl.ds(start, count), :]

    def send_mid(n, s):
        size = part + 2 * wide[n]
        now = grad_of(n, s)
        for ct in range(ct_n):
            gradbf[ct, 0:size, :] = now(ct, 0, size).astype(BF)
        if s == 0:
            loaded("expand", n)
        for jt in range(jt_n):
            total = None
            for ct in range(ct_n):
                term = lax.dot_general(
                    gradbf[ct, 0:size, :],
                    expand[n, 0, jt * LANES : (jt + 1) * LANES, ct * TILE : (ct + 1) * TILE],
                    NT, preferred_element_type=F32,
                )
                total = term if total is None else total + term
            ms[n, s, jt, 0:size, :] = total.astype(BF)
            mid_copy(n, s, jt).start()
        total = None
        for ct in range(ct_n):
            term = lax.dot_general(
                gradbf[ct, 0:size, :], expand[n, 1, :, ct * TILE : (ct + 1) * TILE],
                NT, preferred_element_type=F32,
            )
            total = term if total is None else total + term
        mp[s, 0:size, :] = total

    def slope_of_pre(n):
        pre_copy(n).wait()

        def body(r, _):
            at_rows = pl.ds(pl.multiple_of(r * STEP, STEP), STEP)
            keep = inside(r * STEP - wide[n], STEP, half)
            value = pp[n, at_rows, :] + pr[n, at_rows, :].astype(F32)
            pp[n, at_rows, :] = jnp.where(keep, gelu_slope(value), 0.0)
            return 0

        lax.fori_loop(0, (rows + 2 * wide[n]) // STEP, body, 0)

    def slope_of_saved(n):
        base = (saved[n] - outs[n]) // STEP * STEP

        def body(r, _):
            from_rows = pl.ds(pl.multiple_of(r * STEP + base, STEP), STEP)
            at_rows = pl.ds(pl.multiple_of(r * STEP, STEP), STEP)
            for ct in range(ct_n):
                value = sv[n][from_rows, ct * TILE : (ct + 1) * TILE].astype(F32)
                ss[ct, at_rows, :] = gelu_slope(value)
            return 0

        skew = (saved[n] - outs[n]) % STEP
        lax.fori_loop(0, up(rows + 2 * outs[n] + skew, STEP) // STEP, body, 0)

    def send_back(n, s):
        size = part + 2 * wide[n]
        for jt in range(jt_n):
            lanes_at = slice(jt * LANES, (jt + 1) * LANES)
            mid_copy(n, s, jt).wait()
            go[n, s, jt, 0:size, :] = (
                (mp[s, 0:size, lanes_at] + mr[n, s, jt, 0:size, :].astype(F32))
                * pp[n, s * part : s * part + size, lanes_at]
            ).astype(BF)
            back_copy(n, s, jt).start()

    def finish(n, s):
        size, size_out = part + 2 * wide[n], part + 2 * outs[n]
        shift = wide[n] - outs[n]
        begins = [shift + (1 - t) * dil[n] for t in range(taps)]
        for jt in range(jt_n):
            gpf[0:size, jt * LANES : (jt + 1) * LANES] = go[n, s, jt, 0:size, :].astype(F32)
        left = jnp.concatenate([gpf[k : k + size_out, :].astype(BF) for k in begins], axis=1)
        for ct in range(ct_n):
            acc[ct, 0:size_out, :] = lax.dot_general(
                left, conv[n, 1, ct * TILE : (ct + 1) * TILE, :], NT, preferred_element_type=F32
            )
        for jt in range(jt_n):
            back_copy(n, s, jt).wait()
            gpf[0:size, 0:LANES] = gr[n, s, jt, 0:size, :].astype(F32)
            left = jnp.concatenate([gpf[k : k + size_out, 0:LANES].astype(BF) for k in begins], axis=1)
            for ct in range(ct_n):
                right = jnp.concatenate(
                    [
                        conv[n, 0, ct * TILE : (ct + 1) * TILE, t * half + jt * LANES : t * half + (jt + 1) * LANES]
                        for t in range(taps)
                    ],
                    axis=1,
                )
                acc[ct, 0:size_out, :] += lax.dot_general(left, right, NT, preferred_element_type=F32)
        now = grad_of(n, s)
        later = grads[(top - n + 1) % 2]
        skew = (saved[n] - outs[n]) % STEP
        for ct in range(ct_n):
            total = now(ct, shift, size_out) + acc[ct, 0:size_out, :] * ss[ct, pl.ds(s * part + skew, size_out), :]
            if n:
                later[s, ct, 0:size_out, :] = total
            else:
                out_ref[s * part : (s + 1) * part, ct * TILE : (ct + 1) * TILE] = total.astype(BF)

    for s in range(STREAMS):
        send_mid(top, s)
    for n in reversed(range(layers)):
        slope_of_pre(n)
        for s in range(STREAMS):
            send_back(n, s)
        slope_of_saved(n)
        for s in range(STREAMS):
            finish(n, s)
            if n:
                send_mid(n - 1, s)


def per_device(
    inputs_saved,
    conv_weight,
    expand_weight,
    head_weight,
    batch_of,
    erase_left,
    erase_right,
    bin_gradient,
    cover_bins,
):
    npos, nhead = lax.axis_size("pos"), lax.axis_size("head")
    chan_place = lax.axis_index("chan")
    layers, rows, width = inputs_saved.shape
    taps, inner = conv_weight.shape[1], conv_weight.shape[3]
    exps, cover = cover_bins.shape

    projected = jnp.dot(head_weight, erase_left, preferred_element_type=F32)
    columns = jnp.arange(erase_left.shape[1]) // RANK
    chosen = (columns[None, :] == batch_of[:, None]).astype(F32)
    right_share = lax.dynamic_slice_in_dim(erase_right, chan_place * width, width, 0)
    weight_share = lax.dynamic_slice_in_dim(head_weight, chan_place * width, width, 1)
    removed_rows = jnp.dot(
        projected * chosen, right_share.astype(F32).T, precision=lax.Precision.HIGHEST
    )
    vectors = (weight_share.astype(F32) - removed_rows).astype(BF)

    def fold(array):
        return array.astype(BF).T.reshape(2, cover // 2, exps).transpose(1, 0, 2).reshape(cover // 2, 2 * exps)

    words = jnp.concatenate(
        [fold(cover_bins // 256), fold(cover_bins % 256), fold(bin_gradient), jnp.zeros((exps - 3 * cover // 2, 2 * exps), BF)]
    )
    pay = jnp.concatenate([vectors, words], axis=1)

    wide, _, saved = frames(layers)
    most = rows + 2 * wide[-1]
    span = rows + 2 * saved[-1]
    part = rows // STREAMS
    short = part + 2 * wide[-1]
    ct_n, half = width // TILE, inner // 2
    jt_n = half // LANES
    nx = npos // 2
    sems = pltpu.SemaphoreType.DMA
    return pl.pallas_call(
        functools.partial(kernel, layers, rows, width, inner, taps, npos, nhead, exps),
        out_shape=jax.ShapeDtypeStruct((rows, width), BF),
        in_specs=[pl.BlockSpec(memory_space=pl.ANY)] * 4,
        out_specs=pl.BlockSpec(memory_space=pltpu.VMEM),
        scratch_shapes=[
            *[pltpu.VMEM((rows + 2 * k, width), BF) for k in saved],
            pltpu.VMEM((layers, 2, width, taps * half), BF),
            pltpu.VMEM((layers, 2, half, width), BF),
            pltpu.VMEM((npos, nhead, *pay.shape), BF),
            pltpu.VMEM((most, 4 * exps), BF),
            pltpu.VMEM((ct_n, span, TILE), F32),
            pltpu.VMEM((taps * ct_n, most, TILE), BF),
            pltpu.VMEM((layers, most, half), F32),
            pltpu.VMEM((layers, most, half), BF),
            pltpu.VMEM((layers, most, half), BF),
            pltpu.VMEM((STREAMS, short, half), F32),
            pltpu.VMEM((layers, STREAMS, jt_n, short, LANES), BF),
            pltpu.VMEM((layers, STREAMS, jt_n, short, LANES), BF),
            pltpu.VMEM((layers, STREAMS, jt_n, short, LANES), BF),
            pltpu.VMEM((layers, STREAMS, jt_n, short, LANES), BF),
            pltpu.VMEM((ct_n, most, TILE), F32),
            pltpu.VMEM((ct_n, most, TILE), F32),
            pltpu.VMEM((STREAMS, ct_n, short, TILE), F32),
            pltpu.VMEM((STREAMS, ct_n, short, TILE), F32),
            pltpu.VMEM((ct_n, short, TILE), F32),
            pltpu.VMEM((ct_n, short, TILE), BF),
            pltpu.VMEM((short, half), F32),
            sems((layers * (3 + 2 * taps),)),
            sems,
            sems((layers, 2)), sems((layers, 2)),
            sems((nhead,)), sems((nhead,)),
            sems((nhead,)), sems((nhead,)),
            sems((nx, nhead)), sems((nx, nhead)),
            sems((nx, nhead)), sems((nx, nhead)),
            sems((layers,)), sems((layers,)),
            sems((layers, STREAMS, jt_n)), sems((layers, STREAMS, jt_n)),
            sems((layers, STREAMS, jt_n)), sems((layers, STREAMS, jt_n)),
        ],
        compiler_params=pltpu.CompilerParams(
            collective_id=0, has_side_effects=True, vmem_limit_bytes=63 * 2**20
        ),
    )(inputs_saved, conv_weight, expand_weight, pay)


def solution(mesh):
    return jax.shard_map(
        per_device,
        mesh=mesh,
        in_specs=(
            P(None, ("pos", "head"), "chan"),
            P(None, None, "chan", None),
            P(None, None, "chan"),
            P(("pos", "head"), None),
            P(("pos", "head")),
            P(),
            P(),
            P(("pos", "head"), None),
            P(("pos", "head"), None),
        ),
        out_specs=P(("pos", "head"), "chan"),
        check_vma=False,
    )
```

```python
import functools

import jax
import jax.numpy as jnp
from jax import lax
from jax.experimental import pallas as pl
from jax.experimental.pallas import tpu as pltpu
from jax.sharding import PartitionSpec as P

BASE_DILATION = 4
RANK = 8
SEQ = ("pos", "head")
MESH = pl.DeviceIdType.MESH
BF = jnp.bfloat16
F32 = jnp.float32
TILE = 256
STEP = 16
LANES = 128
STREAMS = 2
NT = (((1,), (1,)), ((), ()))


def gelu_value(value):
    return 0.5 * value * (1.0 + lax.erf(value * 0.7071067811865476))


def gelu_slope(value):
    return (
        0.5 * (1.0 + lax.erf(value * 0.7071067811865476))
        + value * jnp.exp(-0.5 * value * value) * 0.3989422804014327
    )


def up(value, unit):
    return -(-value // unit) * unit


def frames(layers):
    wide, out, saved, before = [], [], [], 0
    for n in range(layers):
        dilation = BASE_DILATION * 2**n
        out.append(before)
        before = up(before + dilation, 8)
        wide.append(before)
        saved.append(up(before + dilation, 16))
    return wide, out, saved


def kernel(
    layers, rows, width, inner, taps, npos, nhead, exps,
    inputs_ref, conv_ref, expand_ref, pay_ref,
    out_ref,
    sv0, sv1, sv2, conv, expand, vall, sbuf, actf, aw, pp, ps, pr, mp, ms, mr, go, gr,
    ss, top_grad, ga, gb, acc, gradbf, gpf,
    load_sem, own_sem, halo_s, halo_r, s1, r1, s2p, r2p, s2x, r2x, s3, r3,
    ps_s, ps_r, ms_s, ms_r, go_s, go_r,
):
    sv = [sv0, sv1, sv2]
    wide, outs, saved = frames(layers)
    dil = [BASE_DILATION * 2**n for n in range(layers)]
    members = npos * nhead
    p, h = lax.axis_index("pos"), lax.axis_index("head")
    mine = lax.axis_index("chan")
    peer = {"chan": 1 - mine}
    place = p * nhead + h
    after = lax.rem(place + 1, members)
    ahead = lax.rem(place + members - 1, members)
    follow = {"pos": after // nhead, "head": lax.rem(after, nhead)}
    precede = {"pos": ahead // nhead, "head": lax.rem(ahead, nhead)}
    mate = p + 1 - 2 * lax.rem(p, 2)
    partner = {"pos": mate}
    nx = npos // 2
    ct_n, half = width // TILE, inner // 2
    jt_n = half // LANES
    halves = [pl.multiple_of((1 - mine) * half, LANES), pl.multiple_of(mine * half, LANES)]

    def remote(src, dst, send, recv, device):
        return pltpu.make_async_remote_copy(
            src_ref=src, dst_ref=dst, send_sem=send, recv_sem=recv, device_id=device, device_id_type=MESH
        )

    def head_of(dh):
        return lax.rem(h + nhead - dh, nhead)

    def pos_of(start, dx):
        return lax.rem(start + npos - 2 * dx, npos)

    loads = {}
    at = 0
    for n in reversed(range(layers)):
        loads["saved", n] = [
            pltpu.make_async_copy(inputs_ref.at[n], sv[n].at[pl.ds(saved[n], rows)], load_sem.at[at])
        ]
        at += 1
        loads["conv", n], loads["expand", n] = [], []
        for side in range(2):
            for t in range(taps):
                loads["conv", n].append(
                    pltpu.make_async_copy(
                        conv_ref.at[n, t, :, pl.ds(halves[side], half)],
                        conv.at[n, side, :, pl.ds(t * half, half)],
                        load_sem.at[at],
                    )
                )
                at += 1
            loads["expand", n].append(
                pltpu.make_async_copy(
                    expand_ref.at[n, pl.ds(halves[side], half)], expand.at[n, side], load_sem.at[at]
                )
            )
            at += 1

    def load(kind, n):
        for copy in loads[kind, n]:
            copy.start()

    def loaded(kind, n):
        for copy in loads[kind, n]:
            copy.wait()

    own = pltpu.make_async_copy(pay_ref, vall.at[p, h], own_sem)
    own.start()
    load("saved", layers - 1)
    load("conv", layers - 1)

    barrier = pltpu.get_barrier_semaphore()
    known = [follow, precede, peer, partner]
    known += [{"head": lax.rem(h + dh, nhead)} for dh in range(1, nhead)]
    known += [{"pos": lax.rem(p + 2 * dx, npos)} for dx in range(1, nx)]
    for device in known:
        pl.semaphore_signal(barrier, inc=1, device_id=device, device_id_type=MESH)
    pl.semaphore_wait(barrier, len(known))

    halos = {}
    for n in reversed(range(layers)):
        k = saved[n]
        halos[n] = [
            remote(inputs_ref.at[n, pl.ds(rows - k, k)], sv[n].at[pl.ds(0, k)],
                   halo_s.at[n, 0], halo_r.at[n, 0], follow),
            remote(inputs_ref.at[n, pl.ds(0, k)], sv[n].at[pl.ds(rows + k, k)],
                   halo_s.at[n, 1], halo_r.at[n, 1], precede),
        ]
    for copy in halos[layers - 1]:
        copy.start()
    first = [
        remote(pay_ref, vall.at[p, h], s1.at[dh], r1.at[dh], {"head": lax.rem(h + dh, nhead)})
        for dh in range(1, nhead)
    ]
    for copy in first:
        copy.start()
    for n in reversed(range(layers - 1)):
        for copy in halos[n]:
            copy.start()
    for n in reversed(range(layers)):
        if n < layers - 1:
            load("saved", n)
            load("conv", n)
        load("expand", n)

    def inside(start, count, lanes):
        spot = place * rows + start + lax.broadcasted_iota(jnp.int32, (count, lanes), 0)
        return (spot >= 0) & (spot < members * rows)

    def make_pre(n):
        size = rows + 2 * wide[n]
        loaded("saved", n)
        for copy in halos[n]:
            copy.wait()

        def activate(r, _):
            place_at = pl.ds(pl.multiple_of(r * STEP, STEP), STEP)
            keep = inside(r * STEP - saved[n], STEP, TILE)
            for ct in range(ct_n):
                value = sv[n][place_at, ct * TILE : (ct + 1) * TILE].astype(F32)
                actf[ct, place_at, :] = jnp.where(keep, gelu_value(value), 0.0)
            return 0

        lax.fori_loop(0, (rows + 2 * saved[n]) // STEP, activate, 0)
        for t in range(taps):
            begin = saved[n] - wide[n] + (t - 1) * dil[n]
            for ct in range(ct_n):
                aw[t * ct_n + ct, 0:size, :] = actf[ct, begin : begin + size, :].astype(BF)
        loaded("conv", n)

        for side in range(2):
            total = None
            for t in range(taps):
                for ct in range(ct_n):
                    term = jnp.dot(
                        aw[t * ct_n + ct, 0:size, :],
                        conv[n, side, ct * TILE : (ct + 1) * TILE, t * half : (t + 1) * half],
                        preferred_element_type=F32,
                    )
                    total = term if total is None else total + term
            if side == 0:
                ps[n, 0:size, :] = total.astype(BF)
                pre_copy(n).start()
            else:
                pp[n, 0:size, :] = total

    def pre_copy(n):
        size = pl.ds(0, rows + 2 * wide[n])
        return remote(ps.at[n, size], pr.at[n, size], ps_s.at[n], ps_r.at[n], peer)

    def chunk(frame, s):
        first_row = s * part + 2 * frame if s else 0
        return first_row, (s + 1) * part + 2 * frame - first_row

    def mid_copy(n, s, jt):
        at_rows = pl.ds(*chunk(wide[n], s))
        return remote(ms.at[n, jt, at_rows], mr.at[n, jt, at_rows], ms_s.at[n, s, jt], ms_r.at[n, s, jt], peer)

    def back_copy(n, s, jt):
        at_rows = pl.ds(*chunk(wide[n], s))
        return remote(go.at[n, jt, at_rows], gr.at[n, jt, at_rows], go_s.at[n, s, jt], go_r.at[n, s, jt], peer)

    part = rows // STREAMS
    top = layers - 1
    make_pre(top)

    own.wait()
    to_mate, to_x = [], []
    for dh in range(nhead):
        if dh:
            first[dh - 1].wait()
        block = vall.at[p, head_of(dh)]
        for dx in range(1, nx):
            copy = remote(block, block, s2x.at[dx, dh], r2x.at[dx, dh], {"pos": lax.rem(p + 2 * dx, npos)})
            copy.start()
            to_x.append((dx, dh, copy))
        copy = remote(block, block, s2p.at[dh], r2p.at[dh], partner)
        copy.start()
        to_mate.append(copy)

    if layers > 1:
        make_pre(top - 1)

    size_top = rows + 2 * wide[top]

    def clear(r, _):
        at_rows = pl.ds(pl.multiple_of(r * STEP, STEP), STEP)
        for ct in range(ct_n):
            top_grad[ct, at_rows, :] = jnp.zeros((STEP, TILE), F32)
        return 0

    lax.fori_loop(0, size_top // STEP, clear, 0)
    lanes = 2 * exps
    part_rows = size_top // 3

    def add_slab(slab):
        def pair(i, _):
            values = []
            for side in range(2):
                a = 2 * i + side
                words = vall[slab, a, :, width : width + lanes].astype(F32)
                spots = words[0:16] * 256.0 + words[16:32]
                heights = words[32:48]
                for rt in range(3):
                    line = (place * rows - wide[top] + rt * part_rows).astype(F32)
                    row = line + lax.broadcasted_iota(jnp.int32, (part_rows, lanes), 0).astype(F32)
                    found = jnp.zeros((part_rows, lanes), F32)
                    for k in range(16):
                        found = found + jnp.where(spots[k : k + 1] == row, heights[k : k + 1], 0.0)
                    sbuf[rt * part_rows : (rt + 1) * part_rows, side * lanes : (side + 1) * lanes] = (
                        found.astype(BF)
                    )
                block = vall[slab, a, :, 0:width]
                values += [block, block]
            right = jnp.concatenate(values, axis=0)
            for ct in range(ct_n):
                top_grad[ct, 0:size_top, :] += jnp.dot(
                    sbuf[...], right[:, ct * TILE : (ct + 1) * TILE], preferred_element_type=F32
                )
            return 0

        lax.fori_loop(0, nhead // 2, pair, 0)

    add_slab(p)
    onward = []
    for dx, dh, copy in to_x:
        copy.wait()
        block = vall.at[pos_of(p, dx), head_of(dh)]
        copy = remote(block, block, s3.at[dx, dh], r3.at[dx, dh], partner)
        copy.start()
        onward.append(copy)
    for copy in to_mate:
        copy.wait()
    add_slab(mate)
    for n in reversed(range(top - 1)):
        make_pre(n)
    for dx in range(1, nx):
        add_slab(pos_of(p, dx))
    for copy in onward:
        copy.wait()
    for dx in range(1, nx):
        add_slab(pos_of(mate, dx))

    grads = [top_grad, ga, gb]

    def send_mid(n, s):
        begin, size = chunk(wide[n], s)
        at_rows = slice(begin, begin + size)
        for ct in range(ct_n):
            gradbf[ct, 0:size, :] = grads[top - n][ct, at_rows, :].astype(BF)
        if s == 0:
            loaded("expand", n)
        for jt in range(jt_n):
            total = None
            for ct in range(ct_n):
                term = lax.dot_general(
                    gradbf[ct, 0:size, :],
                    expand[n, 0, jt * LANES : (jt + 1) * LANES, ct * TILE : (ct + 1) * TILE],
                    NT, preferred_element_type=F32,
                )
                total = term if total is None else total + term
            ms[n, jt, at_rows, :] = total.astype(BF)
            mid_copy(n, s, jt).start()
        total = None
        for ct in range(ct_n):
            term = lax.dot_general(
                gradbf[ct, 0:size, :], expand[n, 1, :, ct * TILE : (ct + 1) * TILE],
                NT, preferred_element_type=F32,
            )
            total = term if total is None else total + term
        mp[at_rows, :] = total

    def slope_of_pre(n):
        pre_copy(n).wait()

        def body(r, _):
            at_rows = pl.ds(pl.multiple_of(r * STEP, STEP), STEP)
            keep = inside(r * STEP - wide[n], STEP, half)
            value = pp[n, at_rows, :] + pr[n, at_rows, :].astype(F32)
            pp[n, at_rows, :] = jnp.where(keep, gelu_slope(value), 0.0)
            return 0

        lax.fori_loop(0, (rows + 2 * wide[n]) // STEP, body, 0)

    def slope_of_saved(n):
        base = (saved[n] - outs[n]) // STEP * STEP

        def body(r, _):
            from_rows = pl.ds(pl.multiple_of(r * STEP + base, STEP), STEP)
            at_rows = pl.ds(pl.multiple_of(r * STEP, STEP), STEP)
            for ct in range(ct_n):
                value = sv[n][from_rows, ct * TILE : (ct + 1) * TILE].astype(F32)
                ss[ct, at_rows, :] = gelu_slope(value)
            return 0

        skew = (saved[n] - outs[n]) % STEP
        lax.fori_loop(0, up(rows + 2 * outs[n] + skew, STEP) // STEP, body, 0)

    def send_back(n, s):
        begin, size = chunk(wide[n], s)
        at_rows = slice(begin, begin + size)
        for jt in range(jt_n):
            lanes_at = slice(jt * LANES, (jt + 1) * LANES)
            mid_copy(n, s, jt).wait()
            go[n, jt, at_rows, :] = (
                (mp[at_rows, lanes_at] + mr[n, jt, at_rows, :].astype(F32)) * pp[n, at_rows, lanes_at]
            ).astype(BF)
            back_copy(n, s, jt).start()

    def taps_of(n, s, source, jt):
        begin, size = chunk(outs[n], s)
        shift = wide[n] - outs[n]
        low, high = begin + shift - dil[n], begin + shift + dil[n] + size
        low, high = low // STEP * STEP, up(high, STEP)
        gpf[0 : high - low, :] = source[n, jt, low:high, :].astype(F32)
        starts = [begin + shift + (1 - t) * dil[n] - low for t in range(taps)]
        return jnp.concatenate([gpf[k : k + size, :].astype(BF) for k in starts], axis=1)

    def weights_of(n, side, ct, jt):
        return jnp.concatenate(
            [
                conv[n, side, ct * TILE : (ct + 1) * TILE, t * half + jt * LANES : t * half + (jt + 1) * LANES]
                for t in range(taps)
            ],
            axis=1,
        )

    def own_half(n, s):
        begin, size = chunk(outs[n], s)
        left = jnp.concatenate([taps_of(n, s, go, jt) for jt in range(jt_n)], axis=1)
        for ct in range(ct_n):
            right = jnp.concatenate([weights_of(n, 1, ct, jt) for jt in range(jt_n)], axis=1)
            acc[ct, begin : begin + size, :] = lax.dot_general(left, right, NT, preferred_element_type=F32)

    def finish(n, s):
        begin, size = chunk(outs[n], s)
        at_rows = slice(begin, begin + size)
        for jt in range(jt_n):
            back_copy(n, s, jt).wait()
            left = taps_of(n, s, gr, jt)
            for ct in range(ct_n):
                acc[ct, at_rows, :] += lax.dot_general(
                    left, weights_of(n, 0, ct, jt), NT, preferred_element_type=F32
                )
        shift = wide[n] - outs[n]
        skew = (saved[n] - outs[n]) % STEP
        for ct in range(ct_n):
            total = (
                grads[top - n][ct, begin + shift : begin + shift + size, :]
                + acc[ct, at_rows, :] * ss[ct, begin + skew : begin + skew + size, :]
            )
            if n:
                grads[top - n + 1][ct, at_rows, :] = total
            else:
                out_ref[at_rows, ct * TILE : (ct + 1) * TILE] = total.astype(BF)

    for s in range(STREAMS):
        send_mid(top, s)
    for n in reversed(range(layers)):
        slope_of_pre(n)
        for s in range(STREAMS):
            send_back(n, s)
        own_half(n, 0)
        slope_of_saved(n)
        for s in range(1, STREAMS):
            own_half(n, s)
        for s in range(STREAMS):
            finish(n, s)
            if n:
                send_mid(n - 1, s)


def per_device(
    inputs_saved,
    conv_weight,
    expand_weight,
    head_weight,
    batch_of,
    erase_left,
    erase_right,
    bin_gradient,
    cover_bins,
):
    npos, nhead = lax.axis_size("pos"), lax.axis_size("head")
    chan_place = lax.axis_index("chan")
    layers, rows, width = inputs_saved.shape
    taps, inner = conv_weight.shape[1], conv_weight.shape[3]
    exps, cover = cover_bins.shape

    projected = jnp.dot(head_weight, erase_left, preferred_element_type=F32)
    columns = jnp.arange(erase_left.shape[1]) // RANK
    chosen = (columns[None, :] == batch_of[:, None]).astype(F32)
    right_share = lax.dynamic_slice_in_dim(erase_right, chan_place * width, width, 0)
    weight_share = lax.dynamic_slice_in_dim(head_weight, chan_place * width, width, 1)
    removed_rows = jnp.dot(
        projected * chosen, right_share.astype(F32).T, precision=lax.Precision.HIGHEST
    )
    vectors = (weight_share.astype(F32) - removed_rows).astype(BF)

    def fold(array):
        return array.astype(BF).T.reshape(2, cover // 2, exps).transpose(1, 0, 2).reshape(cover // 2, 2 * exps)

    words = jnp.concatenate(
        [fold(cover_bins // 256), fold(cover_bins % 256), fold(bin_gradient), jnp.zeros((exps - 3 * cover // 2, 2 * exps), BF)]
    )
    pay = jnp.concatenate([vectors, words], axis=1)

    wide, _, saved = frames(layers)
    most = rows + 2 * wide[-1]
    span = rows + 2 * saved[-1]
    part = rows // STREAMS
    short = part + 2 * wide[-1]
    ct_n, half = width // TILE, inner // 2
    jt_n = half // LANES
    nx = npos // 2
    sems = pltpu.SemaphoreType.DMA
    return pl.pallas_call(
        functools.partial(kernel, layers, rows, width, inner, taps, npos, nhead, exps),
        out_shape=jax.ShapeDtypeStruct((rows, width), BF),
        in_specs=[pl.BlockSpec(memory_space=pl.ANY)] * 4,
        out_specs=pl.BlockSpec(memory_space=pltpu.VMEM),
        scratch_shapes=[
            *[pltpu.VMEM((rows + 2 * k, width), BF) for k in saved],
            pltpu.VMEM((layers, 2, width, taps * half), BF),
            pltpu.VMEM((layers, 2, half, width), BF),
            pltpu.VMEM((npos, nhead, *pay.shape), BF),
            pltpu.VMEM((most, 4 * exps), BF),
            pltpu.VMEM((ct_n, span, TILE), F32),
            pltpu.VMEM((taps * ct_n, most, TILE), BF),
            pltpu.VMEM((layers, most, half), F32),
            pltpu.VMEM((layers, most, half), BF),
            pltpu.VMEM((layers, most, half), BF),
            pltpu.VMEM((most, half), F32),
            pltpu.VMEM((layers, jt_n, most, LANES), BF),
            pltpu.VMEM((layers, jt_n, most, LANES), BF),
            pltpu.VMEM((layers, jt_n, most, LANES), BF),
            pltpu.VMEM((layers, jt_n, most, LANES), BF),
            pltpu.VMEM((ct_n, most, TILE), F32),
            pltpu.VMEM((ct_n, most, TILE), F32),
            pltpu.VMEM((ct_n, most, TILE), F32),
            pltpu.VMEM((ct_n, most, TILE), F32),
            pltpu.VMEM((ct_n, most, TILE), F32),
            pltpu.VMEM((ct_n, short, TILE), BF),
            pltpu.VMEM((most, LANES), F32),
            sems((layers * (3 + 2 * taps),)),
            sems,
            sems((layers, 2)), sems((layers, 2)),
            sems((nhead,)), sems((nhead,)),
            sems((nhead,)), sems((nhead,)),
            sems((nx, nhead)), sems((nx, nhead)),
            sems((nx, nhead)), sems((nx, nhead)),
            sems((layers,)), sems((layers,)),
            sems((layers, STREAMS, jt_n)), sems((layers, STREAMS, jt_n)),
            sems((layers, STREAMS, jt_n)), sems((layers, STREAMS, jt_n)),
        ],
        compiler_params=pltpu.CompilerParams(
            collective_id=0, has_side_effects=True, vmem_limit_bytes=63 * 2**20
        ),
    )(inputs_saved, conv_weight, expand_weight, pay)


def solution(mesh):
    return jax.shard_map(
        per_device,
        mesh=mesh,
        in_specs=(
            P(None, ("pos", "head"), "chan"),
            P(None, None, "chan", None),
            P(None, None, "chan"),
            P(("pos", "head"), None),
            P(("pos", "head")),
            P(),
            P(),
            P(("pos", "head"), None),
            P(("pos", "head"), None),
        ),
        out_specs=P(("pos", "head"), "chan"),
        check_vma=False,
    )
```
